32 devices in a mesh: groups: 2 (over x), tensor: 8 (over z, y), store: 2 (over core).
Axes of the slice: x: 2, y: 2, z: 4, core: 2. Of those that a mesh axis runs over, the one named last changes fastest.
Arguments:
- hidden: bfloat16 [3072, 29568], P(('groups', 'store'), 'tensor'), parts along dimension 0, may hold values from -6 to 6
- request_adapter: int32 [128], P(('groups', 'store')), parts along dimension 0, may hold values from 0 to 47
- down_weight: bfloat16 [29568, 8192], P('tensor'), may hold values from -0.046875 to 0.046875
- adapter_input_factors: bfloat16 [48, 29568, 64], P('store', 'tensor'), may hold values from -0.03125 to 0.03125
- adapter_output_factors: bfloat16 [48, 64, 8192], P('store', None, 'tensor'), may hold values from -0.75 to 0.75
Outputs:
- projected: bfloat16 [3072, 8192], P(('groups', 'store'), 'tensor'), parts along dimension 0
The draws below stay inside these ranges and needn't reach their ends.
There are 2 independent parts, one for each index of `groups`. The reference program is written for one: setup_inputs(seed, part) draws one part's arguments, and reference() takes and returns one part's arrays. A program takes and returns all parts, laid end to end along the dimension named above; an argument that names none is the same for every part. Nothing has to cross between parts.
All inputs are finite; a program needn't handle non-finite values.
Results may differ from the reference program's by a relative error of at most 0.0033.
Values may be sent and summed in bfloat16 or wider, within the bound.
A program may use at most 320 MiB of HBM per device.

```python
import math
import jax
import jax.numpy as jnp
import numpy as np
from jax import lax

MODEL_WIDTH = 8192
HIDDEN_UNITS = 29568
ADAPTER_RANK = 64
ADAPTER_TOTAL = 48
CAND = 4
DRAFT = 6
REQUESTS = 64
ROWS = 1536


def touch_ends(entries, key, least, top_value):
    extent = entries.shape
    index_at = [jax.random.randint(jax.random.fold_in(key, axis), (), 0, extent[axis]) for axis in range(len(extent))]
    entries = entries.at[tuple(index_at)].set(least)
    longest = extent.index(max(extent))
    index_at[longest] = (index_at[longest] + 1) % extent[longest]
    return entries.at[tuple(index_at)].set(top_value)


def with_spikes(array, own_key, source, target, shards_of, factor):
    def block_of(axis_at):
        return (jnp.arange(array.shape[axis_at]) // (array.shape[axis_at] // shards_of)).reshape((-1,) + (1,) * (array.ndim - 1 - axis_at))

    one_side = jax.random.permutation(own_key, shards_of)[block_of(target)]
    other_side = (block_of(target) + shards_of // 2) % shards_of
    return jnp.where((block_of(source) == one_side) | (block_of(source) == other_side), factor * array, array)


def levels(key, shape, pieces, low, largest):
    level = 1.0
    for axis_at, shards_of in pieces:
        draws = jax.random.uniform(jax.random.fold_in(jax.random.fold_in(key, 6), axis_at), (shards_of,), jnp.float32, low / len(pieces), largest / len(pieces))
        level = level * jnp.repeat(jnp.exp(draws), shape[axis_at] // shards_of).reshape((-1,) + (1,) * (len(shape) - 1 - axis_at))
    return level


def rank_bounds(amount, lean):
    loads = [(1 << 20) // math.isqrt(standing ** lean) + 1 for standing in range(1, amount + 1)]
    deviation = 1 + sum(loads) // (1 << 30)
    return np.cumsum(np.array([max(1, weight // deviation) for weight in loads]))


def ranked(rng, extent, count, lean):
    grid = rank_bounds(count, lean)
    pick = jax.random.randint(jax.random.fold_in(rng, 1), extent, 0, int(grid[count - 1]))
    rank = jnp.searchsorted(jnp.asarray(grid, jnp.int32), pick, side="right")
    return jax.random.permutation(jax.random.fold_in(rng, 2), count)[rank].astype(jnp.int32)


def noise(key, dims, spread, limit, shards=(), kind=jnp.bfloat16):
    factor_of = levels(key, dims, shards, -0.22, 0.18) if shards else 1.0
    drawn = jax.random.normal(key, dims, jnp.float32) * spread * factor_of
    return jnp.minimum(jnp.maximum(drawn, -limit), limit).astype(kind)


def heavy_noise(key, extent, width, limit, pieces, heavy, dtype=jnp.bfloat16):
    values = width * jax.random.normal(key, extent, jnp.float32)
    if pieces:
        values = values * levels(key, extent, pieces, -0.22, 0.18)
    return jnp.clip(with_spikes(values, jax.random.fold_in(key, 3), *heavy), -limit, limit).astype(dtype)


def setup_inputs(seed: int = 0, part: int = 0) -> dict:
    key_of = jax.random.split(jax.random.key(seed), 6)
    part_keys = jax.random.split(jax.random.fold_in(key_of[5], part), 6)
    return {
        "hidden": noise(part_keys[0], (ROWS, HIDDEN_UNITS), 1.0, 6.0, ((0, 2), (1, 8))),
        "request_adapter": touch_ends(ranked(part_keys[1], (REQUESTS,), ADAPTER_TOTAL, 2), jax.random.fold_in(part_keys[1], 3), 0, ADAPTER_TOTAL - 1).astype(jnp.int32),
        "down_weight": heavy_noise(key_of[2], (HIDDEN_UNITS, MODEL_WIDTH), HIDDEN_UNITS ** -0.5, 0.046875, ((0, 8),), (0, 1, 8, 2.0)),
        "adapter_input_factors": noise(key_of[3], (ADAPTER_TOTAL, HIDDEN_UNITS, ADAPTER_RANK), HIDDEN_UNITS ** -0.5, 0.03125, ((0, 2), (1, 8))),
        "adapter_output_factors": noise(key_of[4], (ADAPTER_TOTAL, ADAPTER_RANK, MODEL_WIDTH), ADAPTER_RANK ** -0.5, 0.75, ((0, 2), (2, 8))),
    }


def reference(hidden, request_adapter, down_weight, adapter_input_factors, adapter_output_factors):
    base = jnp.dot(hidden, down_weight, preferred_element_type=jnp.float32)
    per_request = CAND * DRAFT
    grouped = hidden.reshape(REQUESTS, per_request, HIDDEN_UNITS)

    def one_request(pair):
        rows_block, selected_adapter = pair
        input_factor = lax.dynamic_index_in_dim(adapter_input_factors, selected_adapter, 0, keepdims=False)
        output_factor = lax.dynamic_index_in_dim(adapter_output_factors, selected_adapter, 0, keepdims=False)
        low = jnp.dot(rows_block, input_factor, preferred_element_type=jnp.float32).astype(jnp.bfloat16)
        return jnp.dot(low, output_factor, preferred_element_type=jnp.float32)

    adapted = lax.map(one_request, (grouped, request_adapter.astype(jnp.int32)))
    return (base + adapted.reshape(ROWS, MODEL_WIDTH)).astype(jnp.bfloat16)
```

```python
import functools

import jax
import jax.numpy as jnp
from jax import lax
from jax.experimental import pallas as pl
from jax.experimental.pallas import tpu as pltpu
from jax.sharding import PartitionSpec as P

PIECES = 2
ROW_TILE = 256
LANES = 256


def exchange(block, bit, devices):
    return lax.ppermute(block, "tensor", [(i, i ^ bit) for i in range(devices)])


def per_request_kernel(count, contract, chosen_ref, rows_ref, *refs):
    del chosen_ref
    out_ref = refs[-1]
    step = rows_ref.shape[0] // count
    for at in range(count):
        part = slice(at * step, (at + 1) * step)
        out_ref[part, :] = lax.dot_general(
            rows_ref[part, :], refs[at][0], (((1,), (contract,)), ((), ())),
            preferred_element_type=jnp.float32,
        )


def per_request(rows, request_adapter, factor, contract, after=()):
    total, depth = rows.shape
    requests = request_adapter.shape[0]
    count = next(n for n in (8, 4, 2, 1) if requests % n == 0)
    step = count * (total // requests)
    made = factor.shape[2 - contract]

    def chosen_block(at):
        return pl.BlockSpec((1,) + factor.shape[1:], lambda i, chosen: (chosen[i * count + at], 0, 0))

    def kernel(chosen_ref, rows_ref, *refs):
        per_request_kernel(count, contract, chosen_ref, rows_ref, *refs[:count], refs[-1])

    return pl.pallas_call(
        kernel,
        out_shape=jax.ShapeDtypeStruct((total, made), jnp.float32),
        grid_spec=pltpu.PrefetchScalarGridSpec(
            num_scalar_prefetch=1,
            grid=(requests // count,),
            in_specs=[pl.BlockSpec((step, depth), lambda i, chosen: (i, 0))]
            + [chosen_block(at) for at in range(count)]
            + [pl.BlockSpec(memory_space=pl.ANY)] * len(after),
            out_specs=pl.BlockSpec((step, made), lambda i, chosen: (i, 0)),
        ),
        compiler_params=pltpu.CompilerParams(vmem_limit_bytes=32 * 1024 * 1024),
        cost_estimate=pl.CostEstimate(
            flops=2 * total * depth * made,
            bytes_accessed=2 * (rows.size + requests * factor.shape[1] * factor.shape[2]) + 4 * total * made,
            transcendentals=0,
        ),
    )(request_adapter, rows, *[factor] * count, *after)


def low_part(hidden, request_adapter, input_factor, after=()):
    return per_request(hidden, request_adapter, jnp.swapaxes(input_factor, 1, 2), 1, after)


def adapt(rank_total, request_adapter, output_factor, after=()):
    return per_request(rank_total.astype(jnp.bfloat16), request_adapter, output_factor, 0, after)


def product_kernel(counts, blocks, place_ref, hidden_ref, weight_ref, *refs):
    jobs = len(counts)
    columns, arrival = refs[-2], refs[-1]
    outs = refs[-2 - jobs:-2]
    _, halves, _, lanes = columns.shape
    copies = {}
    for job in range(jobs):
        for half in range(halves):
            at = pl.multiple_of((place_ref[blocks[job]] * halves + half) * lanes, lanes)
            copies[job, half] = pltpu.make_async_copy(
                weight_ref.at[:, pl.ds(at, lanes)], columns.at[job, half], arrival.at[job, half]
            )
            copies[job, half].start()
    rows = hidden_ref.shape[0]
    tile = ROW_TILE if rows % ROW_TILE == 0 else rows
    seen = 0
    for job in range(jobs):
        added = refs[seen:seen + counts[job]]
        seen += counts[job]
        for half in range(halves):
            copies[job, half].wait()
            place = slice(half * lanes, (half + 1) * lanes)
            for at in range(rows // tile):
                part = slice(at * tile, (at + 1) * tile)
                total = jnp.dot(
                    hidden_ref[part, :], columns[job, half], preferred_element_type=jnp.float32
                )
                for ref in added:
                    total += ref[part, place].astype(jnp.float32)
                outs[job][part, place] = total.astype(jnp.bfloat16)


def product(hidden, down_weight, places, blocks, piece, added, after=()):
    rows, depth = hidden.shape
    jobs = len(added)
    lanes = min(LANES, piece)
    whole = pl.BlockSpec(memory_space=pltpu.VMEM)
    anywhere = pl.BlockSpec(memory_space=pl.ANY)
    flat = [array for job in added for array in job]
    return pl.pallas_call(
        functools.partial(product_kernel, [len(job) for job in added], blocks),
        out_shape=[jax.ShapeDtypeStruct((rows, piece), jnp.bfloat16)] * jobs,
        in_specs=[pl.BlockSpec(memory_space=pltpu.SMEM), whole, anywhere]
        + [whole] * len(flat)
        + [anywhere] * len(after),
        out_specs=[whole] * jobs,
        scratch_shapes=[
            pltpu.VMEM((jobs, piece // lanes, depth, lanes), down_weight.dtype),
            pltpu.SemaphoreType.DMA((jobs, piece // lanes)),
        ],
        compiler_params=pltpu.CompilerParams(vmem_limit_bytes=40 * 1024 * 1024),
        cost_estimate=pl.CostEstimate(
            flops=2 * jobs * rows * depth * piece,
            bytes_accessed=2 * (rows * depth + jobs * (depth * piece + rows * piece)),
            transcendentals=0,
        ),
    )(places, hidden, down_weight, *flat, *after)


def halved(hidden, request_adapter, down_weight, input_factor, output_factor, devices):
    me = lax.axis_index("tensor")
    width = output_factor.shape[2]
    piece = width // PIECES
    order = [(d, k) for k in range(PIECES) for d in (6, 4)]
    order += [(d, k) for d in (2, 0) for k in range(PIECES)]
    distance = jnp.arange(devices, dtype=jnp.int32)
    places = ((me ^ distance)[:, None] * PIECES + jnp.arange(PIECES, dtype=jnp.int32)).reshape(-1)
    arrived, second, third, out = {}, {}, {}, [None] * PIECES
    after = ()
    adapted = None

    def parts(at):
        d, k = order[at]
        added = [arrived[at]]
        if d == 4:
            added.append(second[4, k])
        if d == 0:
            added += [second[0, k], third[k], adapted[:, k * piece:(k + 1) * piece]]
        return added

    def run(*jobs):
        blocks, added = [], []
        for kind, at in jobs:
            d, k = order[at]
            blocks.append((d if kind == "keep" else d ^ 1) * PIECES + k)
            added.append(parts(at) if kind == "keep" else [])
        made = product(hidden, down_weight, places, blocks, piece, added, after)
        for (kind, at), block in zip(jobs, made):
            d, k = order[at]
            if kind == "send":
                arrived[at] = exchange(block, 1, devices)
            elif d in (6, 2):
                second[d ^ 2, k] = exchange(block, 2, devices)
            elif d == 4:
                third[k] = exchange(block, 4, devices)
            else:
                out[k] = block
        return (made[0],)

    def behind(value):
        return lax.optimization_barrier((value, *after))[0]

    after = run(("send", 0))
    after = run(("send", 1), ("send", 2))
    after = run(("keep", 0), ("send", 3))
    part = low_part(hidden, request_adapter, input_factor, after)
    after = (part,)
    parts_low = lax.all_gather(part, "tensor", axis=0)
    after = run(("keep", 1), ("send", 4))
    after = run(("keep", 2), ("send", 5))
    after = run(("keep", 3), ("send", 6))
    after = run(("keep", 4), ("send", 7))
    part = jnp.sum(behind(parts_low), axis=0)
    adapted = adapt(part, request_adapter, output_factor, after)
    after = (adapted,)
    after = run(("keep", 5))
    after = run(("keep", 6))
    run(("keep", 7))
    return jnp.concatenate(out, axis=1)


def on_device(devices, hidden, request_adapter, down_weight, adapter_input_factors, adapter_output_factors):
    input_factor = lax.all_gather(adapter_input_factors, "store", axis=0, tiled=True)
    output_factor = lax.all_gather(adapter_output_factors, "store", axis=0, tiled=True)
    if devices == 8:
        return halved(hidden, request_adapter, down_weight, input_factor, output_factor, devices)
    rank_total = lax.psum(low_part(hidden, request_adapter, input_factor), "tensor")
    adapted = adapt(rank_total, request_adapter, output_factor)
    partial = lax.dot_general(
        down_weight, hidden, (((0,), (1,)), ((), ())), preferred_element_type=jnp.float32
    )
    summed = lax.psum_scatter(partial, "tensor", scatter_dimension=0, tiled=True).T
    return (summed + adapted).astype(jnp.bfloat16)


def solution(mesh):
    in_specs = (
        P(("groups", "store"), "tensor"),
        P(("groups", "store")),
        P("tensor", None),
        P("store", "tensor", None),
        P("store", None, "tensor"),
    )
    out_specs = P(("groups", "store"), "tensor")
    return jax.shard_map(
        functools.partial(on_device, mesh.shape["tensor"]),
        mesh=mesh, in_specs=in_specs, out_specs=out_specs, check_vma=False,
    )
```
